768 devices in a mesh: dom: 48 (over x, z), grp: 16 (over y, core).
Axes of the slice: x: 4, y: 8, z: 12, core: 2. Of those that a mesh axis runs over, the one named last changes fastest.
Arguments:
- node_features: bfloat16 [1572864, 256], P(('dom', 'grp')), may hold values from -6 to 6
- edge_blocks: bfloat16 [18432, 128, 128], P(('dom', 'grp')), may hold values from -0.375 to 0.375
- block_target: int32 [768, 24], P(('dom', 'grp')), may hold values from 0 to 15
- block_source: int32 [768, 24], P(('dom', 'grp')), may hold values from 0 to 15
- block_count: int32 [768], P(('dom', 'grp')), may hold values from 1 to 24, as said below
- replica_rows: int32 [768, 48, 16], P(('dom', 'grp')), may hold values from 1280 to 2047, as said below
- master_rows: int32 [768, 48, 16], P(('dom', 'grp')), may hold values from 0 to 1279
- send_counts: int32 [768, 48], P(('dom', 'grp')), may hold values from 0 to 16, as said below
- bin_delay: int32 [768, 48, 2], P(('dom', 'grp')), may hold values from 0 to 2
- past_partials: bfloat16 [768, 2, 48, 16, 256], P(('dom', 'grp')), may hold values from -6 to 6
- self_weight: bfloat16 [256, 256], replicated, may hold values from -0.375 to 0.375
- neighbor_weight: bfloat16 [256, 256], replicated, may hold values from -0.375 to 0.375
- output_cotangent: bfloat16 [1572864, 256], P(('dom', 'grp')), may hold values from -6 to 6
Outputs:
- layer_output: bfloat16 [1572864, 256], P(('dom', 'grp'))
- self_gradient: float32 [256, 256], replicated
- neighbor_gradient: float32 [256, 256], replicated
The draws below stay inside these ranges and needn't reach their ends.
Inputs may be any that keep to these rules, and one draw needn't show every extreme that they name: `block_count`: some partition has all 24 edge blocks live. `replica_rows`: for each partition every local row from 1280 to 2047 appears exactly once. `send_counts`: every partition has a peer with all 16 slots live.
All inputs are finite; a program needn't handle non-finite values.
Results may differ from the reference program's by a relative error of at most 0.01.
The reference program's roundings to bfloat16 on the way count: a program that leaves them out, or rounds other values in their place, can miss the bound.
Values sent between devices are 32-bit elements; how exact they have to be, the bound alone decides.
A program may use at most 32 MiB of HBM per device.

```python
import math
import jax
import jax.numpy as jnp
from jax import lax

F = 256
BS = 128
NODE_DEV = 2048
NBLK = 24
SLOTS = 16
BIN = 8
DELAY = 2
TILES = 16
NBIN = 2
MROWS = 1280
NODES = 1572864
N_DOM = 48
N_GRP = 16
DEVICES = 768


def draw_block_count(key, part):
    key = jax.random.fold_in(key, 11)
    first_key, second_key = jax.random.split(key)
    counts = jax.random.randint(first_key, (DEVICES,), 1, NBLK + 1)
    fullest = jax.random.randint(second_key, (), 0, DEVICES)
    counts = jnp.where(jnp.arange(DEVICES) == fullest, NBLK, counts)
    return counts.astype(jnp.int32)


def draw_replica_rows(key, part):
    key = jax.random.fold_in(key, 23)
    device_keys = jax.random.split(key, DEVICES)
    orders = jax.vmap(lambda single: jax.random.permutation(single, N_DOM * SLOTS))(device_keys)
    return (orders + MROWS).reshape(DEVICES, N_DOM, SLOTS).astype(jnp.int32)


def draw_send_counts(key, part):
    key = jax.random.fold_in(key, 37)
    first_key, second_key = jax.random.split(key)
    counts = jax.random.randint(first_key, (DEVICES, N_DOM), 0, SLOTS + 1)
    fullest = jax.random.randint(second_key, (DEVICES, 1), 0, N_DOM)
    counts = jnp.where(jnp.arange(N_DOM)[None, :] == fullest, SLOTS, counts)
    return counts.astype(jnp.int32)


def set_ends(array, own_key, low, high):
    longest = array.shape.index(max(array.shape))
    spots = []
    for shift in (0, 1):
        where = [jax.random.randint(jax.random.fold_in(own_key, axis), (), 0, length) for axis, length in enumerate(array.shape)]
        where[longest] = (where[longest] + shift) % array.shape[longest]
        spots.append(tuple(where))
    return array.at[spots[0]].set(low).at[spots[1]].set(high)


def steps_of(stream_key, extent, pieces, low, largest):
    gain = 1.0
    for position, shards_of in pieces:
        heights = jax.random.uniform(jax.random.fold_in(jax.random.fold_in(stream_key, 6), position), (shards_of,), jnp.float32, low / len(pieces), largest / len(pieces))
        gain = gain * jnp.repeat(jnp.exp(heights), extent[position] // shards_of).reshape((-1,) + (1,) * (len(extent) - 1 - position))
    return gain


def noise(rng, extent, scale, reach, shards=(), kind=jnp.bfloat16):
    gain = steps_of(rng, extent, shards, -0.22, 0.18) if shards else 1.0
    drawn = jax.random.normal(rng, extent, jnp.float32) * scale * gain
    return jnp.minimum(jnp.maximum(drawn, -reach), reach).astype(kind)


def setup_inputs(seed: int = 0) -> dict:
    arg_keys = jax.random.split(jax.random.key(seed), 14)
    return {
        "node_features": noise(arg_keys[0], (NODES, F), 1.0, 6.0, ((0, 768),)),
        "edge_blocks": noise(arg_keys[1], (DEVICES * NBLK, BS, BS), (2 * BS) ** -0.5, 0.375, ((0, 768),)),
        "block_target": set_ends(jax.random.randint(arg_keys[2], (DEVICES, NBLK), 0, TILES), jax.random.fold_in(arg_keys[2], 1), 0, TILES - 1).astype(jnp.int32),
        "block_source": set_ends(jax.random.randint(arg_keys[3], (DEVICES, NBLK), 0, TILES), jax.random.fold_in(arg_keys[3], 1), 0, TILES - 1).astype(jnp.int32),
        "block_count": draw_block_count(jax.random.fold_in(arg_keys[13], 71), 0),
        "replica_rows": draw_replica_rows(jax.random.fold_in(arg_keys[13], 71), 0),
        "master_rows": set_ends(jax.random.randint(arg_keys[6], (DEVICES, N_DOM, SLOTS), 0, MROWS), jax.random.fold_in(arg_keys[6], 1), 0, MROWS - 1).astype(jnp.int32),
        "send_counts": draw_send_counts(jax.random.fold_in(arg_keys[13], 71), 0),
        "bin_delay": set_ends(jax.random.randint(arg_keys[8], (DEVICES, N_DOM, NBIN), 0, DELAY + 1), jax.random.fold_in(arg_keys[8], 1), 0, DELAY).astype(jnp.int32),
        "past_partials": noise(arg_keys[9], (DEVICES, DELAY, N_DOM, SLOTS, F), 1.0, 6.0, ((0, 768),)),
        "self_weight": noise(arg_keys[10], (F, F), F ** -0.5, 0.375),
        "neighbor_weight": noise(arg_keys[11], (F, F), F ** -0.5, 0.375),
        "output_cotangent": noise(arg_keys[12], (NODES, F), 1.0, 6.0, ((0, 768),)),
    }


def aggregate(features, blocks, targets, sources, count):
    tile_stack = features.reshape(TILES, BS, F)
    gathered = tile_stack[sources]
    products = jnp.einsum('bij,bjf->bif', blocks.astype(jnp.float32), gathered.astype(jnp.float32), precision=lax.Precision.HIGHEST)
    in_use = (jnp.arange(NBLK, dtype=jnp.int32) < count).astype(jnp.float32)
    summed = jnp.zeros((TILES, BS, F), jnp.float32).at[targets].add(products * in_use[:, None, None])
    return summed.reshape(NODE_DEV, F)

def swap_peers(values):
    shape = values.shape
    arranged = values.reshape((N_DOM, N_GRP) + shape[1:])
    arranged = jnp.swapaxes(arranged, 0, 2)
    return arranged.reshape(shape)

def slot_state(counts, delays):
    slot_live = (jnp.arange(SLOTS, dtype=jnp.int32)[None, :] < counts[:, None])[:, :, None]
    slot_delay = jnp.repeat(delays, BIN, axis=1)[:, :, None]
    return (slot_live, slot_delay)

def send_phase(inputs):
    features, blocks, targets, sources, count, replicas, counts, delays, history = inputs
    partial_value = aggregate(features, blocks, targets, sources, count)
    fresh_rows = partial_value[replicas.reshape(-1)].reshape(N_DOM, SLOTS, F)
    slot_live, slot_delay = slot_state(counts, delays)
    stale_rows = jnp.zeros((N_DOM, SLOTS, F), jnp.float32)
    for epoch_back in range(DELAY):
        stale_rows = jnp.where(slot_delay == epoch_back + 1, history[epoch_back].astype(jnp.float32), stale_rows)
    outgoing = jnp.where(slot_live, jnp.where(slot_delay == 0, fresh_rows, stale_rows), jnp.zeros_like(stale_rows))
    return (partial_value, outgoing)

def master_phase(inputs):
    partial_value, masters, incoming = inputs
    totals = partial_value.at[masters.reshape(-1)].add(incoming.reshape(-1, F))
    return totals[masters.reshape(-1)].reshape(N_DOM, SLOTS, F)

def layer_phase(inputs):
    partial_value, masters, incoming, replicas, counts, delays, answer, features, cotangent, self_weight, neighbor_weight = inputs
    totals = partial_value.at[masters.reshape(-1)].add(incoming.reshape(-1, F))
    fresh_rows = partial_value[replicas.reshape(-1)].reshape(N_DOM, SLOTS, F)
    slot_live, slot_delay = slot_state(counts, delays)
    merged = totals.at[replicas.reshape(-1)].set(jnp.where(slot_live, answer, fresh_rows).reshape(-1, F))
    rounded = merged.astype(jnp.bfloat16)
    preact = jnp.dot(features, self_weight, preferred_element_type=jnp.float32) + jnp.dot(rounded, neighbor_weight, preferred_element_type=jnp.float32)
    positive = preact > 0
    output = jnp.where(positive, preact, jnp.zeros_like(preact)).astype(jnp.bfloat16)
    masked = jnp.where(positive, cotangent, jnp.zeros_like(cotangent))
    self_part = jnp.dot(features.T, masked, preferred_element_type=jnp.float32)
    neighbor_part = jnp.dot(rounded.T, masked, preferred_element_type=jnp.float32)
    return (output, self_part, neighbor_part)

def reference(node_features, edge_blocks, block_target, block_source, block_count, replica_rows, master_rows, send_counts, bin_delay, past_partials, self_weight, neighbor_weight, output_cotangent):
    features = node_features.reshape(DEVICES, NODE_DEV, F)
    blocks = edge_blocks.reshape(DEVICES, NBLK, BS, BS)
    cotangent = output_cotangent.reshape(DEVICES, NODE_DEV, F)
    partials, outgoing = lax.map(send_phase, (features, blocks, block_target, block_source, block_count, replica_rows, send_counts, bin_delay, past_partials))
    incoming = swap_peers(outgoing)
    replies = lax.map(master_phase, (partials, master_rows, incoming))
    answers = swap_peers(replies)

    def with_weights(inputs):
        return layer_phase(inputs + (self_weight, neighbor_weight))
    outputs, self_parts, neighbor_parts = lax.map(with_weights, (partials, master_rows, incoming, replica_rows, send_counts, bin_delay, answers, features, cotangent))
    factor = 1.0 / math.sqrt(NODES)
    return (outputs.reshape(NODES, F), lax.optimization_barrier(jnp.sum(self_parts, axis=0)) * factor, lax.optimization_barrier(jnp.sum(neighbor_parts, axis=0)) * factor)
```

```python
import functools
import math

import jax
import jax.numpy as jnp
from jax import lax
from jax.experimental import pallas as pl
from jax.experimental.pallas import tpu as pltpu
from jax.sharding import PartitionSpec as P

MESH = pl.DeviceIdType.MESH
VM = pl.BlockSpec(memory_space=pltpu.VMEM)

def a2a_kernel(nchunk, x_ref, o_ref, ssem, rsem, lsem):
    n = x_ref.shape[1]
    dom = lax.axis_index("dom"); grp = lax.axis_index("grp")
    bar = pltpu.get_barrier_semaphore()
    def sig(k, _):
        pl.semaphore_signal(bar, inc=1, device_id=(lax.rem(dom + k, n), grp), device_id_type=MESH)
        return 0
    lax.fori_loop(1, n, sig, 0)
    pl.semaphore_wait(bar, n - 1)
    for c in range(nchunk):
        def send(k, _):
            p = lax.rem(dom + k, n)
            pltpu.make_async_remote_copy(src_ref=x_ref.at[c, p], dst_ref=o_ref.at[c, n - k],
                send_sem=ssem.at[c], recv_sem=rsem.at[c], device_id=(p, grp), device_id_type=MESH).start()
            return 0
        lax.fori_loop(1, n, send, 0)
    for c in range(nchunk):
        o_ref[c, 0] = x_ref[c, dom]
    for c in range(nchunk):
        w = o_ref.at[c, pl.ds(1, n - 1)]
        pltpu.make_async_copy(w, w, rsem.at[c]).wait()
    for c in range(nchunk):
        w = o_ref.at[c, pl.ds(1, n - 1)]
        pltpu.make_async_copy(w, w, ssem.at[c]).wait()

def a2a(x, cid=0):
    nc = x.shape[0]
    return pl.pallas_call(functools.partial(a2a_kernel, nc), out_shape=jax.ShapeDtypeStruct(x.shape, x.dtype),
        in_specs=[VM], out_specs=VM,
        scratch_shapes=[pltpu.SemaphoreType.DMA((nc,)), pltpu.SemaphoreType.DMA((nc,)), pltpu.SemaphoreType.DMA],
        compiler_params=pltpu.CompilerParams(collective_id=cid, has_side_effects=True, vmem_limit_bytes=48*2**20), name=f"a2a{nc}")(x)

def ar_kernel(nx, ny, nz, factor, g_ref, o_ref, acc, b0, b1, b2, b3, acc1, acc2, ssem, rsem):
    dom = lax.axis_index("dom"); grp = lax.axis_index("grp")
    x = dom // nz; z = lax.rem(dom, nz); y = grp // 2; core = lax.rem(grp, 2)
    bar = pltpu.get_barrier_semaphore()
    partner = (dom, y * 2 + 1 - core)
    xp = lambda k: (lax.rem(x + k, nx) * nz + z, grp)
    yp = lambda k: (dom, lax.rem(y + k, ny) * 2 + core)
    zp = lambda k: (x * nz + lax.rem(z + k, nz), grp)
    def sig(d): pl.semaphore_signal(bar, inc=1, device_id=d, device_id_type=MESH)
    sig(partner)
    for f, m in ((xp, nx), (yp, ny), (zp, nz)):
        for k in range(1, m): sig(f(k))
    pl.semaphore_wait(bar, 1 + nx - 1 + ny - 1 + nz - 1)
    H = g_ref.shape[0] // 2; X = H // nx; Y = X // ny
    def cp(s, d, st, dev):
        pltpu.make_async_remote_copy(src_ref=s, dst_ref=d, send_sem=ssem.at[st], recv_sem=rsem.at[st], device_id=dev, device_id_type=MESH).start()
    def wt(ref, sem):
        pltpu.make_async_copy(ref, ref, sem).wait()
    al = pl.multiple_of
    mine = pl.ds(al(core * H, H), H); other = pl.ds(al((1 - core) * H, H), H)
    cp(g_ref.at[other], b0, 0, partner)
    wt(b0, rsem.at[0])
    acc[...] = g_ref[mine] + b0[...]
    for k in range(1, nx):
        cp(acc.at[pl.ds(al(lax.rem(x + k, nx) * X, X), X)], b1.at[k - 1], 1, xp(k))
    wt(b1, rsem.at[1])
    acc1[...] = acc[pl.ds(al(x * X, X), X)] + b1[0] + b1[1] + b1[2]
    for k in range(1, ny):
        cp(acc1.at[pl.ds(al(lax.rem(y + k, ny) * Y, Y), Y)], b2.at[k - 1], 2, yp(k))
    wt(b2, rsem.at[2])
    s = acc1[pl.ds(al(y * Y, Y), Y)]
    for k in range(ny - 1): s = s + b2[k]
    acc2[...] = s
    for k in range(1, nz):
        cp(acc2, b3.at[z], 3, zp(k))
    b3[z] = s
    w = b3.at[pl.ds(0, nz - 1)]
    wt(w, rsem.at[3])
    s = b3[0]
    for k in range(1, nz): s = s + b3[k]
    row = al(core * H + x * X + y * Y, Y)
    o_ref[pl.ds(row, Y)] = s * factor
    piece = o_ref.at[pl.ds(row, Y)]
    for k in range(1, ny): cp(piece, piece, 4, yp(k))
    w4 = o_ref.at[pl.ds(0, Y * (ny - 1))]
    wt(w4, rsem.at[4])
    blk = o_ref.at[pl.ds(al(core * H + x * X, X), X)]
    for k in range(1, nx): cp(blk, blk, 5, xp(k))
    w5 = o_ref.at[pl.ds(0, X * (nx - 1))]
    wt(w5, rsem.at[5])
    half = o_ref.at[mine]
    cp(half, half, 6, partner)
    wt(half, rsem.at[6])
    wt(b0, ssem.at[0]); wt(b1, ssem.at[1]); wt(b2, ssem.at[2]); wt(w, ssem.at[3]); wt(w4, ssem.at[4]); wt(w5, ssem.at[5]); wt(half, ssem.at[6])

def allreduce(g, nx, ny, nz, factor, cid=1):
    R, C = g.shape
    H = R // 2; X = H // nx; Y = X // ny
    f = jnp.float32
    return pl.pallas_call(functools.partial(ar_kernel, nx, ny, nz, factor), out_shape=jax.ShapeDtypeStruct(g.shape, f),
        in_specs=[VM], out_specs=VM,
        scratch_shapes=[pltpu.VMEM((H, C), f), pltpu.VMEM((H, C), f), pltpu.VMEM((nx - 1, X, C), f), pltpu.VMEM((ny - 1, Y, C), f),
            pltpu.VMEM((nz, Y, C), f), pltpu.VMEM((X, C), f), pltpu.VMEM((Y, C), f), pltpu.SemaphoreType.DMA((7,)), pltpu.SemaphoreType.DMA((7,))],
        compiler_params=pltpu.CompilerParams(collective_id=cid, has_side_effects=True, vmem_limit_bytes=48*2**20), name="ar")(g)


def aggregate(node_features, edge_blocks, block_target, block_source, block_count):
    node_rows, feat_width = node_features.shape
    tile_size = edge_blocks.shape[1]
    tile_count = node_rows // tile_size
    block_total = edge_blocks.shape[0]
    tile_stack = node_features.reshape(tile_count, tile_size, feat_width)
    gathered = jnp.take(tile_stack, block_source[0], axis=0)
    products = jnp.einsum("bij,bjf->bif", edge_blocks, gathered, preferred_element_type=jnp.float32)
    in_use = (lax.broadcasted_iota(jnp.int32, (block_total,), 0) < block_count[0]).astype(
        jnp.float32
    )
    summed = (
        jnp.zeros((tile_count, tile_size, feat_width), jnp.float32)
        .at[block_target[0]]
        .add(products * in_use[:, None, None])
    )
    return summed.reshape(node_rows, feat_width)


def layer_rows(features, aggregate_rows, cotangent, self_weight, neighbor_weight):
    rounded = aggregate_rows.astype(jnp.bfloat16)
    preact = jnp.dot(features, self_weight, preferred_element_type=jnp.float32) + jnp.dot(
        rounded, neighbor_weight, preferred_element_type=jnp.float32
    )
    positive = preact > 0
    output = jnp.where(positive, preact, jnp.zeros_like(preact)).astype(jnp.bfloat16)
    masked = jnp.where(positive, cotangent, jnp.zeros_like(cotangent))
    contract_rows = (((0,), (0,)), ((), ()))
    self_part = lax.dot_general(features, masked, contract_rows, preferred_element_type=jnp.float32)
    neighbor_part = lax.dot_general(
        rounded, masked, contract_rows, preferred_element_type=jnp.float32
    )
    return (output, self_part, neighbor_part)


def shards(
    node_features,
    edge_blocks,
    block_target,
    block_source,
    block_count,
    replica_rows,
    master_rows,
    send_counts,
    bin_delay,
    past_partials,
    self_weight,
    neighbor_weight,
    output_cotangent,
):
    node_rows, feat_width = node_features.shape
    peer_count = replica_rows.shape[1]
    slot_count = replica_rows.shape[2]
    bin_width = slot_count // bin_delay.shape[2]
    replica_flat = replica_rows[0].reshape(-1)
    master_flat = master_rows[0].reshape(-1)
    slot_live = (
        lax.broadcasted_iota(jnp.int32, (peer_count, slot_count), 1) < send_counts[0][:, None]
    )[:, :, None]
    slot_delay = jnp.repeat(bin_delay[0], bin_width, axis=1)[:, :, None]
    history = past_partials[0]
    stale_rows = jnp.zeros((peer_count, slot_count, feat_width), jnp.float32)
    for epoch_back in range(history.shape[0]):
        stale_rows = jnp.where(
            slot_delay == epoch_back + 1, history[epoch_back].astype(jnp.float32), stale_rows
        )
    partial_value = aggregate(node_features, edge_blocks, block_target, block_source, block_count)
    fresh_rows = jnp.take(partial_value, replica_flat, axis=0).reshape(
        peer_count, slot_count, feat_width
    )
    outgoing = jnp.where(
        slot_live, jnp.where(slot_delay == 0, fresh_rows, stale_rows), jnp.zeros_like(stale_rows)
    )
    order = lax.rem(lax.axis_index("dom") + jnp.arange(peer_count), peer_count)
    back = lax.rem(jnp.arange(peer_count) - lax.axis_index("dom") + peer_count, peer_count)
    incoming = a2a(outgoing[None])[0]
    master_rel = master_rows[0][order].reshape(-1)
    totals = partial_value.at[master_rel].add(incoming.reshape(-1, feat_width))
    reply = jnp.take(totals, master_flat, axis=0).reshape(peer_count, slot_count, feat_width)
    answer = a2a(reply[None])[0][back]
    merged = totals.at[replica_flat].set(
        jnp.where(slot_live, answer, fresh_rows).reshape(-1, feat_width)
    )
    layer_output, self_local, neighbor_local = layer_rows(
        node_features, merged, output_cotangent, self_weight, neighbor_weight
    )
    node_total = node_rows * lax.axis_size("dom") * lax.axis_size("grp")
    factor = 1.0 / math.sqrt(node_total)
    total = allreduce(jnp.concatenate([self_local, neighbor_local]), 4, 8, 12, factor)
    return (layer_output, total[:feat_width], total[feat_width:])


def solution(mesh):
    return jax.shard_map(
        shards,
        mesh=mesh,
        in_specs=(
            P(("dom", "grp"), None),
            P(("dom", "grp"), None, None),
            P(("dom", "grp"), None),
            P(("dom", "grp"), None),
            P(("dom", "grp")),
            P(("dom", "grp"), None, None),
            P(("dom", "grp"), None, None),
            P(("dom", "grp"), None),
            P(("dom", "grp"), None, None),
            P(("dom", "grp"), None, None, None, None),
            P(),
            P(),
            P(("dom", "grp"), None),
        ),
        out_specs=(P(("dom", "grp"), None), P(), P()),
        check_vma=False,
    )
```

```python
import functools
import math

import jax
import jax.numpy as jnp
from jax import lax
from jax.experimental import pallas as pl
from jax.experimental.pallas import tpu as pltpu
from jax.sharding import PartitionSpec as P

MESH = pl.DeviceIdType.MESH
F32 = jnp.float32
BF16 = jnp.bfloat16
NX, NY, NZ = 4, 8, 12
LANES = 128
CHUNKS = 2


def three_parts(x):
    high = x.astype(BF16)
    rest = x - high.astype(F32)
    middle = rest.astype(BF16)
    low = (rest - middle.astype(F32)).astype(BF16)
    return jnp.concatenate([high, middle, low], axis=1)


def add_parts(d):
    return d[:, :LANES] + d[:, LANES : 2 * LANES] + d[:, 2 * LANES :]


def one_hot(hit):
    return jnp.where(hit, 1.0, 0.0).astype(BF16)


def dot(a, b):
    return jnp.dot(a, b, preferred_element_type=F32)


def wait_bytes(ref, sem):
    pltpu.make_async_copy(ref, ref, sem).wait()


def layer_kernel(
    factor, masters,
    weight, source, nf_h, eb_h, hist_h, rows_h, ws_h, wn_h, cot_h,
    out, self_grad, neighbor_grad,
    nf, eb, hist, cols, rows, ws, wn, cot,
    prod, partial, pick, scat, take, place, live_row, outg, inc, rep, ans, aggr,
    pre, lhs, g, b0, acc, b1, acc1, b2, acc2, b3, grad,
    in_sem, x_send, x_recv, r_send, r_recv,
):
    dom = lax.axis_index("dom")
    grp = lax.axis_index("grp")
    x, z, y, core = dom // NZ, lax.rem(dom, NZ), grp // 2, lax.rem(grp, 2)
    peers = NX * NZ
    slots = cols.shape[0] // peers
    total_slots = cols.shape[0]
    tiles, tile, feat = nf.shape
    nodes = tiles * tile
    late = nodes - masters
    blocks = eb.shape[0]

    def x_peer(k):
        return (lax.rem(x + k, NX) * NZ + z, grp)

    def y_peer(k):
        return (dom, lax.rem(y + k, NY) * 2 + core)

    def z_peer(k):
        return (x * NZ + lax.rem(z + k, NZ), grp)

    partner = (dom, y * 2 + 1 - core)

    barrier = pltpu.get_barrier_semaphore()

    def greet(device):
        pl.semaphore_signal(barrier, inc=1, device_id=device, device_id_type=MESH)

    def greet_dom(k, _):
        greet((lax.rem(dom + k, peers), grp))
        return 0

    lax.fori_loop(1, peers, greet_dom, 0)
    for k in range(1, NY):
        greet(y_peer(k))
    greet(partner)

    loads = [
        pltpu.make_async_copy(a, b, in_sem.at[n])
        for n, (a, b) in enumerate(
            ((eb_h, eb), (nf_h, nf), (rows_h, rows), (hist_h, hist), (ws_h, ws), (wn_h, wn), (cot_h, cot))
        )
    ]
    for copy in loads:
        copy.start()
    loads[0].wait()
    loads[1].wait()

    def multiply(b, _):
        prod[b] = dot(eb[b], nf[source[0, b]])
        return 0

    lax.fori_loop(0, blocks, multiply, 0)

    def collect(t, _):
        total = jnp.zeros((tile, feat), F32)
        for b in range(blocks):
            total = total + weight[t, b] * prod[b]
        partial[pl.ds(pl.multiple_of(t * tile, tile), tile), :] = total
        return 0

    lax.fori_loop(masters // tile, nodes // tile, collect, 0)
    loads[2].wait()
    loads[3].wait()
    cols[...] = rows[...].T

    def make_pick(i, _):
        part = pl.ds(pl.multiple_of(i * LANES, LANES), LANES)
        number = lax.broadcasted_iota(jnp.int32, (LANES, late), 1) + masters
        pick[part, :] = one_hot(cols[part, 0:1] == number)
        return 0

    lax.fori_loop(0, total_slots // LANES, make_pick, 0)

    def fill(c):
        lanes = pl.ds(c * LANES, LANES)
        terms = three_parts(partial[pl.ds(masters, late), lanes])

        def piece(i, _):
            part = pl.ds(pl.multiple_of(i * 256, 256), 256)
            fresh = add_parts(dot(pick[part, :], terms))
            age = cols[part, 2:3]
            stale = jnp.where(age == 1, hist[0, part, lanes].astype(F32), 0.0)
            stale = jnp.where(age == 2, hist[1, part, lanes].astype(F32), stale)
            outg[c, part, :] = fresh + stale
            return 0

        lax.fori_loop(0, total_slots // 256, piece, 0)

    def exchange(from_ref, to_ref, c, send, recv):
        mine = pl.ds(pl.multiple_of(dom * slots, slots), slots)

        def start(i, _):
            step, dx = i // NX, NX - 1 - lax.rem(i, NX)
            off = (step + 1) // 2
            dz = NZ // 2 + off * (2 * lax.rem(step, 2) - 1)
            peer = lax.rem(x + dx, NX) * NZ + lax.rem(z + dz, NZ)
            pltpu.make_async_remote_copy(
                src_ref=from_ref.at[c, pl.ds(pl.multiple_of(peer * slots, slots), slots)],
                dst_ref=to_ref.at[c, mine],
                send_sem=send,
                recv_sem=recv,
                device_id=(peer, grp),
                device_id_type=MESH,
            ).start()
            return 0

        lax.fori_loop(0, peers - 1, start, 0)
        to_ref[c, mine, :] = from_ref[c, mine, :]

    def all_but_mine(ref, c):
        return ref.at[c, pl.ds(0, total_slots - slots)]

    fill(0)
    pl.semaphore_wait(barrier, peers - 1 + NY - 1 + 1)
    exchange(outg, inc, 0, x_send.at[0], x_recv.at[0])
    fill(1)
    exchange(outg, inc, 1, x_send.at[1], x_recv.at[1])

    lax.fori_loop(0, masters // tile, collect, 0)
    for copy in loads[4:]:
        copy.wait()

    def make_scat(i, _):
        part = pl.ds(pl.multiple_of(i * LANES, LANES), LANES)
        number = lax.broadcasted_iota(jnp.int32, (LANES, total_slots), 0) + i * LANES
        scat[part, :] = one_hot(rows[3:4, :] == number)
        return 0

    lax.fori_loop(0, masters // LANES, make_scat, 0)

    def make_take(i, _):
        part = pl.ds(pl.multiple_of(i * LANES, LANES), LANES)
        number = lax.broadcasted_iota(jnp.int32, (LANES, masters), 1)
        take[part, :] = one_hot(cols[part, 3:4] == number)
        return 0

    lax.fori_loop(0, total_slots // LANES, make_take, 0)

    def make_place(i, _):
        part = pl.ds(pl.multiple_of(i * LANES, LANES), LANES)
        number = lax.broadcasted_iota(jnp.int32, (LANES, total_slots), 0) + i * LANES + masters
        hits = one_hot(rows[1:2, :] == number)
        place[part, :] = hits
        live_row[part, :] = dot(hits, jnp.ones((total_slots, LANES), BF16))
        return 0

    lax.fori_loop(0, late // LANES, make_place, 0)

    for c in range(CHUNKS):
        lanes = pl.ds(c * LANES, LANES)
        wait_bytes(all_but_mine(inc, c), x_recv.at[c])
        terms = three_parts(inc[c])

        def add_in(i, _):
            part = pl.ds(pl.multiple_of(i * 256, 256), 256)
            totals = partial[part, lanes] + add_parts(dot(scat[part, :], terms))
            aggr[part, lanes] = totals.astype(BF16)
            return 0

        lax.fori_loop(0, masters // 256, add_in, 0)
        rounded = aggr[pl.ds(0, masters), lanes]

        def reply(i, _):
            part = pl.ds(pl.multiple_of(i * 256, 256), 256)
            rep[c, part, :] = dot(take[part, :], rounded)
            return 0

        lax.fori_loop(0, total_slots // 256, reply, 0)
        exchange(rep, ans, c, x_send.at[CHUNKS + c], x_recv.at[CHUNKS + c])

    contract_rows = (((0,), (0,)), ((), ()))
    g[...] = jnp.zeros_like(g)

    def early(i, _):
        part = pl.ds(pl.multiple_of(i * 256, 256), 256)
        features = nf[pl.ds(2 * i, 2)].reshape(2 * tile, feat)
        rounded = aggr[part, :]
        preact = dot(features, ws[...]) + dot(rounded, wn[...])
        out[part, :] = jnp.maximum(preact, 0.0).astype(BF16)
        kept = jnp.where(preact > 0, cot[part, :], jnp.zeros((256, feat), BF16))
        for c in range(CHUNKS):
            side = kept[:, c * LANES : (c + 1) * LANES]
            g[c, pl.ds(0, feat), :] += lax.dot_general(features, side, contract_rows, preferred_element_type=F32)
            g[c, pl.ds(feat, feat), :] += lax.dot_general(rounded, side, contract_rows, preferred_element_type=F32)
        return 0

    lax.fori_loop(0, masters // 256, early, 0)
    end = pl.ds(masters, late)
    features = nf[pl.ds(masters // tile, late // tile)].reshape(late, feat)
    pre[...] = dot(features, ws[...])
    lhs[pl.ds(0, feat), :] = features.T

    for c in range(CHUNKS):
        lanes = pl.ds(c * LANES, LANES)
        wait_bytes(all_but_mine(ans, c), x_recv.at[CHUNKS + c])
        placed = dot(place[...], ans[c].astype(BF16))
        rounded = jnp.where(live_row[...] > 0, placed, partial[end, lanes]).astype(BF16)
        pre[...] += dot(rounded, wn[pl.ds(c * LANES, LANES), :])
        lhs[pl.ds(feat + c * LANES, LANES), :] = rounded.T

    half, x_rows = feat, feat // NX
    y_rows = x_rows // NY
    own = pl.ds(pl.multiple_of(core * half, half), half)
    other = pl.ds(pl.multiple_of((1 - core) * half, half), half)
    x_own = pl.ds(pl.multiple_of(x * x_rows, x_rows), x_rows)
    y_own = pl.ds(pl.multiple_of(y * y_rows, y_rows), y_rows)

    def copy_to(src, dst, stage, c, device):
        pltpu.make_async_remote_copy(
            src_ref=src, dst_ref=dst, send_sem=r_send.at[stage, c], recv_sem=r_recv.at[stage, c],
            device_id=device, device_id_type=MESH,
        ).start()

    for c in range(CHUNKS):
        lanes = pl.ds(c * LANES, LANES)
        preact = pre[:, lanes]
        out[end, lanes] = jnp.maximum(preact, 0.0).astype(BF16)
        kept = jnp.where(preact > 0, cot[end, lanes], jnp.zeros((late, LANES), BF16))
        g[c] = g[c] + dot(lhs[...], kept)
        copy_to(g.at[c, other], b0.at[c], 0, c, partner)
    for c in range(CHUNKS):
        wait_bytes(b0.at[c], r_recv.at[0, c])
        acc[c] = g[c, own, :] + b0[c]
        for k in (2, 1, 3):
            part = pl.ds(pl.multiple_of(lax.rem(x + k, NX) * x_rows, x_rows), x_rows)
            copy_to(acc.at[c, part], b1.at[c, k - 1], 1, c, x_peer(k))
    for c in range(CHUNKS):
        wait_bytes(b1.at[c], r_recv.at[1, c])
        acc1[c] = acc[c, x_own, :] + b1[c, 0] + b1[c, 1] + b1[c, 2]
        for k in (4, 3, 5, 2, 6, 1, 7):
            part = pl.ds(pl.multiple_of(lax.rem(y + k, NY) * y_rows, y_rows), y_rows)
            copy_to(acc1.at[c, part], b2.at[c, k - 1], 2, c, y_peer(k))
    for c in range(CHUNKS):
        wait_bytes(b2.at[c], r_recv.at[2, c])
        total = acc1[c, y_own, :]
        for k in range(NY - 1):
            total = total + b2[c, k]
        acc2[c] = total
        for k in (6, 5, 7, 4, 8, 3, 9, 2, 10, 1, 11):
            copy_to(acc2.at[c], b3.at[c, z], 3, c, z_peer(k))
        b3[c, z] = total
    at = pl.ds(pl.multiple_of(core * half + x * x_rows + y * y_rows, y_rows), y_rows)
    x_block = pl.ds(pl.multiple_of(core * half + x * x_rows, x_rows), x_rows)
    for c in range(CHUNKS):
        lanes = pl.ds(c * LANES, LANES)
        wait_bytes(b3.at[c, pl.ds(0, NZ - 1)], r_recv.at[3, c])
        total = b3[c, 0]
        for k in range(1, NZ):
            total = total + b3[c, k]
        grad[at, lanes] = total * factor
        for k in (4, 3, 5, 2, 6, 1, 7):
            copy_to(grad.at[at, lanes], grad.at[at, lanes], 4, c, y_peer(k))
    for c in range(CHUNKS):
        lanes = pl.ds(c * LANES, LANES)
        wait_bytes(grad.at[pl.ds(0, y_rows * (NY - 1)), lanes], r_recv.at[4, c])
        for k in (2, 1, 3):
            copy_to(grad.at[x_block, lanes], grad.at[x_block, lanes], 5, c, x_peer(k))
    for c in range(CHUNKS):
        lanes = pl.ds(c * LANES, LANES)
        wait_bytes(grad.at[pl.ds(0, x_rows * (NX - 1)), lanes], r_recv.at[5, c])
        copy_to(grad.at[own, lanes], grad.at[own, lanes], 6, c, partner)
    for c in range(CHUNKS):
        lanes = pl.ds(c * LANES, LANES)
        wait_bytes(grad.at[own, lanes], r_recv.at[6, c])
        for n, ref in enumerate((
            b0.at[c], b1.at[c], b2.at[c], b3.at[c, pl.ds(0, NZ - 1)], grad.at[pl.ds(0, y_rows * (NY - 1)), lanes],
            grad.at[pl.ds(0, x_rows * (NX - 1)), lanes], grad.at[own, lanes],
        )):
            wait_bytes(ref, r_send.at[n, c])
        wait_bytes(all_but_mine(inc, c), x_send.at[c])
        wait_bytes(all_but_mine(ans, c), x_send.at[CHUNKS + c])
    self_grad[...] = grad[pl.ds(0, feat), :]
    neighbor_grad[...] = grad[pl.ds(feat, feat), :]


def shards(
    node_features,
    edge_blocks,
    block_target,
    block_source,
    block_count,
    replica_rows,
    master_rows,
    send_counts,
    bin_delay,
    past_partials,
    self_weight,
    neighbor_weight,
    output_cotangent,
):
    nodes, feat = node_features.shape
    _, peers, slots = replica_rows.shape
    total_slots = peers * slots
    bin_width = slots // bin_delay.shape[2]
    masters = nodes - total_slots
    late = total_slots
    live = lax.broadcasted_iota(jnp.int32, (peers, slots), 1) < send_counts[0][:, None]
    delay = jnp.repeat(bin_delay[0], bin_width, axis=1)
    replicas = replica_rows[0]
    fresh_row = jnp.where(live & (delay == 0), replicas, -1)
    live_place = jnp.where(live, replicas, -1)
    age = jnp.where(live, delay, 0)
    both = [fresh_row, live_place, age, master_rows[0]] * 2
    rows = jnp.stack(both).reshape(len(both), total_slots)
    tiles = nodes // edge_blocks.shape[1]
    used = lax.broadcasted_iota(jnp.int32, (1, block_target.shape[1]), 1) < block_count[0]
    into = block_target == lax.broadcasted_iota(jnp.int32, (tiles, block_target.shape[1]), 0)
    weight = jnp.where(used & into, 1.0, 0.0)
    history = past_partials[0].reshape(past_partials.shape[1], total_slots, feat)
    factor = 1.0 / math.sqrt(nodes * lax.axis_size("dom") * lax.axis_size("grp"))

    vmem = pl.BlockSpec(memory_space=pltpu.VMEM)
    smem = pl.BlockSpec(memory_space=pltpu.SMEM)
    hbm = pl.BlockSpec(memory_space=pl.ANY)
    blocks, tile = edge_blocks.shape[:2]
    x_rows = feat // NX
    y_rows = x_rows // NY
    big = (CHUNKS, total_slots, LANES)
    v = pltpu.VMEM
    return pl.pallas_call(
        functools.partial(layer_kernel, factor, masters),
        out_shape=(
            jax.ShapeDtypeStruct((nodes, feat), BF16),
            jax.ShapeDtypeStruct((feat, feat), F32),
            jax.ShapeDtypeStruct((feat, feat), F32),
        ),
        in_specs=[smem] * 2 + [hbm] * 7,
        out_specs=(vmem, vmem, vmem),
        scratch_shapes=[
            v((tiles, tile, feat), BF16), v(edge_blocks.shape, BF16), v(history.shape, BF16), v(rows.shape[::-1], jnp.int32),
            v(rows.shape, jnp.int32), v((feat, feat), BF16), v((feat, feat), BF16), v((nodes, feat), BF16),
            v((blocks, tile, feat), F32), v((nodes, feat), F32),
            v((total_slots, late), BF16), v((masters, total_slots), BF16), v((total_slots, masters), BF16),
            v((late, total_slots), BF16), v((late, LANES), F32),
            v(big, F32), v(big, F32), v(big, F32), v(big, F32), v((nodes, feat), BF16),
            v((late, feat), F32), v((2 * feat, late), BF16),
            v((CHUNKS, 2 * feat, LANES), F32), v((CHUNKS, feat, LANES), F32), v((CHUNKS, feat, LANES), F32),
            v((CHUNKS, NX - 1, x_rows, LANES), F32), v((CHUNKS, x_rows, LANES), F32),
            v((CHUNKS, NY - 1, y_rows, LANES), F32), v((CHUNKS, y_rows, LANES), F32),
            v((CHUNKS, NZ, y_rows, LANES), F32), v((2 * feat, feat), F32),
            pltpu.SemaphoreType.DMA((7,)), pltpu.SemaphoreType.DMA((2 * CHUNKS,)), pltpu.SemaphoreType.DMA((2 * CHUNKS,)),
            pltpu.SemaphoreType.DMA((7, CHUNKS)), pltpu.SemaphoreType.DMA((7, CHUNKS)),
        ],
        compiler_params=pltpu.CompilerParams(
            collective_id=0, has_side_effects=True, vmem_limit_bytes=62 * 2**20
        ),
        name="layer",
    )(
        weight, block_source, node_features.reshape(tiles, tile, feat), edge_blocks, history, rows,
        self_weight, neighbor_weight, output_cotangent,
    )


def solution(mesh):
    return jax.shard_map(
        shards,
        mesh=mesh,
        in_specs=(
            P(("dom", "grp"), None),
            P(("dom", "grp"), None, None),
            P(("dom", "grp"), None),
            P(("dom", "grp"), None),
            P(("dom", "grp")),
            P(("dom", "grp"), None, None),
            P(("dom", "grp"), None, None),
            P(("dom", "grp"), None),
            P(("dom", "grp"), None, None),
            P(("dom", "grp"), None, None, None, None),
            P(),
            P(),
            P(("dom", "grp"), None),
        ),
        out_specs=(P(("dom", "grp"), None), P(), P()),
        check_vma=False,
    )
```

```python
import functools
import math

import jax
import jax.numpy as jnp
from jax import lax
from jax.experimental import pallas as pl
from jax.experimental.pallas import tpu as pltpu
from jax.sharding import PartitionSpec as P

MESH = pl.DeviceIdType.MESH
F32 = jnp.float32
BF16 = jnp.bfloat16
NX, NY, NZ = 4, 8, 12
LANES = 128
CHUNKS = 2


def three_parts(x):
    high = x.astype(BF16)
    rest = x - high.astype(F32)
    middle = rest.astype(BF16)
    low = (rest - middle.astype(F32)).astype(BF16)
    return jnp.concatenate([high, middle, low], axis=1)


def add_parts(d):
    return d[:, :LANES] + d[:, LANES : 2 * LANES] + d[:, 2 * LANES :]


def one_hot(hit):
    return jnp.where(hit, 1.0, 0.0).astype(BF16)


def dot(a, b):
    return jnp.dot(a, b, preferred_element_type=F32)


def wait_bytes(ref, sem):
    pltpu.make_async_copy(ref, ref, sem).wait()


def layer_kernel(
    factor, masters,
    source_h, nf_h, eb_h, hist_h, rep_h, mas_h, sent_h, delay_h, target_h, count, ws_h, wn_h, cot_h,
    out, self_grad, neighbor_grad,
    source, nf, eb, hist, replica, master, sent, delay, target, ws, wn, cot, weight, cols, rows,
    prod, partial, pick, scat, take, place, live_row, outg, inc, rep, ans, aggr,
    pre, lhs, g, b0, acc, b1, acc1, b2, acc2, b3, grad,
    in_sem, x_send, x_recv, r_send, r_recv,
):
    dom = lax.axis_index("dom")
    grp = lax.axis_index("grp")
    x, z, y, core = dom // NZ, lax.rem(dom, NZ), grp // 2, lax.rem(grp, 2)
    peers = NX * NZ
    slots = cols.shape[0] // peers
    total_slots = cols.shape[0]
    tiles, tile, feat = nf.shape
    nodes = tiles * tile
    late = nodes - masters
    blocks = eb.shape[0]

    def x_peer(k):
        return (lax.rem(x + k, NX) * NZ + z, grp)

    def y_peer(k):
        return (dom, lax.rem(y + k, NY) * 2 + core)

    def z_peer(k):
        return (x * NZ + lax.rem(z + k, NZ), grp)

    partner = (dom, y * 2 + 1 - core)

    pairs = (
        (rep_h, replica), (mas_h, master), (sent_h, sent), (delay_h, delay), (target_h, target), (source_h, source),
        (eb_h, eb), (nf_h, nf), (hist_h, hist), (ws_h, ws), (wn_h, wn), (cot_h, cot),
    )
    loads = [pltpu.make_async_copy(a, b, in_sem.at[n]) for n, (a, b) in enumerate(pairs)]
    for copy in loads[:8]:
        copy.start()
    barrier = pltpu.get_barrier_semaphore()

    def greet(device):
        pl.semaphore_signal(barrier, inc=1, device_id=device, device_id_type=MESH)

    def greet_dom(k, _):
        greet((lax.rem(dom + k, peers), grp))
        return 0

    lax.fori_loop(1, peers, greet_dom, 0)
    for k in range(1, NY):
        greet(y_peer(k))
    greet(partner)

    for copy in loads[:5]:
        copy.wait()

    shift = slots.bit_length() - 1

    spread = one_hot(
        lax.broadcasted_iota(jnp.int32, (peers, total_slots), 1) >> shift
        == lax.broadcasted_iota(jnp.int32, (peers, total_slots), 0)
    )
    here = lax.broadcasted_iota(jnp.int32, (slots, total_slots), 1) & (slots - 1) == lax.broadcasted_iota(
        jnp.int32, (slots, total_slots), 0
    )

    def flat(ref):
        high = dot((ref[...] >> 4).astype(F32).astype(BF16), spread)
        low = dot((ref[...] & 15).astype(F32).astype(BF16), spread)
        return jnp.sum(jnp.where(here, high * 16.0 + low, 0.0), axis=0, keepdims=True)

    replica_row, master_row = flat(replica), flat(master)
    sent_row = dot(sent[...].astype(F32).astype(BF16), spread)
    delays = dot(delay[...].astype(F32).astype(BF16), spread)
    slot = lax.broadcasted_iota(jnp.int32, (1, total_slots), 1) & (slots - 1)
    bins = delay.shape[0]
    delay_row = delays[0:1]
    for n in range(1, bins):
        delay_row = jnp.where(slot >= n * (slots // bins), delays[n : n + 1], delay_row)
    live = slot.astype(F32) < sent_row
    rows[0:1, :] = jnp.where(live & (delay_row == 0.0), replica_row, -1.0)
    rows[1:2, :] = jnp.where(live, replica_row, -1.0)
    rows[2:3, :] = jnp.where(live, delay_row, 0.0)
    rows[3:4, :] = master_row
    rows[4:8, :] = jnp.zeros((4, total_slots), F32)
    cols[...] = rows[...].T

    def make_pick(i, _):
        part = pl.ds(pl.multiple_of(i * LANES, LANES), LANES)
        number = (lax.broadcasted_iota(jnp.int32, (LANES, late), 1) + masters).astype(F32)
        pick[part, :] = one_hot(cols[part, 0:1] == number)
        return 0

    lax.fori_loop(0, total_slots // LANES, make_pick, 0)

    used = lax.broadcasted_iota(jnp.int32, (tiles, blocks), 1) < count[0]
    into = lax.broadcasted_iota(jnp.int32, (tiles, blocks), 0) == target[...]
    weight[...] = jnp.where(used & into, 1.0, 0.0)
    for copy in loads[5:8]:
        copy.wait()
    for copy in loads[8:]:
        copy.start()

    def multiply(b, _):
        prod[b] = dot(eb[b], nf[source[0, b]])
        return 0

    lax.fori_loop(0, blocks, multiply, 0, unroll=True)
    def collect(t, _):
        total = jnp.zeros((tile, feat), F32)
        for b in range(blocks):
            total = total + weight[pl.ds(t, 1), pl.ds(b, 1)] * prod[b]
        partial[pl.ds(pl.multiple_of(t * tile, tile), tile), :] = total
        return 0

    lax.fori_loop(masters // tile, nodes // tile, collect, 0)
    def fill(c):
        lanes = pl.ds(c * LANES, LANES)
        terms = three_parts(partial[pl.ds(masters, late), lanes])

        def piece(i, _):
            part = pl.ds(pl.multiple_of(i * 256, 256), 256)
            fresh = add_parts(dot(pick[part, :], terms))
            age = cols[part, 2:3]
            stale = jnp.where(age == 1, hist[0, part, lanes].astype(F32), 0.0)
            stale = jnp.where(age == 2, hist[1, part, lanes].astype(F32), stale)
            outg[c, part, :] = fresh + stale
            return 0

        lax.fori_loop(0, total_slots // 256, piece, 0)

    def exchange(from_ref, to_ref, c, send, recv):
        mine = pl.ds(pl.multiple_of(dom * slots, slots), slots)

        def start(i, _):
            step, dx = i // NX, NX - 1 - lax.rem(i, NX)
            off = (step + 1) // 2
            dz = NZ // 2 + off * (2 * lax.rem(step, 2) - 1)
            peer = lax.rem(x + dx, NX) * NZ + lax.rem(z + dz, NZ)
            pltpu.make_async_remote_copy(
                src_ref=from_ref.at[c, pl.ds(pl.multiple_of(peer * slots, slots), slots)],
                dst_ref=to_ref.at[c, mine],
                send_sem=send,
                recv_sem=recv,
                device_id=(peer, grp),
                device_id_type=MESH,
            ).start()
            return 0

        lax.fori_loop(0, peers - 1, start, 0)
        to_ref[c, mine, :] = from_ref[c, mine, :]

    def all_but_mine(ref, c):
        return ref.at[c, pl.ds(0, total_slots - slots)]

    loads[8].wait()
    fill(0)
    pl.semaphore_wait(barrier, peers - 1 + NY - 1 + 1)
    exchange(outg, inc, 0, x_send.at[0], x_recv.at[0])
    fill(1)
    exchange(outg, inc, 1, x_send.at[1], x_recv.at[1])

    lax.fori_loop(0, masters // tile, collect, 0)
    for copy in loads[9:]:
        copy.wait()

    def make_scat(i, _):
        part = pl.ds(pl.multiple_of(i * LANES, LANES), LANES)
        number = (lax.broadcasted_iota(jnp.int32, (LANES, total_slots), 0) + i * LANES).astype(F32)
        scat[part, :] = one_hot(rows[3:4, :] == number)
        return 0

    lax.fori_loop(0, masters // LANES, make_scat, 0)

    def make_take(i, _):
        part = pl.ds(pl.multiple_of(i * LANES, LANES), LANES)
        number = lax.broadcasted_iota(jnp.int32, (LANES, masters), 1).astype(F32)
        take[part, :] = one_hot(cols[part, 3:4] == number)
        return 0

    lax.fori_loop(0, total_slots // LANES, make_take, 0)

    def make_place(i, _):
        part = pl.ds(pl.multiple_of(i * LANES, LANES), LANES)
        number = (lax.broadcasted_iota(jnp.int32, (LANES, total_slots), 0) + i * LANES + masters).astype(F32)
        hits = one_hot(rows[1:2, :] == number)
        place[part, :] = hits
        live_row[part, :] = dot(hits, jnp.ones((total_slots, LANES), BF16))
        return 0

    lax.fori_loop(0, late // LANES, make_place, 0)

    for c in range(CHUNKS):
        lanes = pl.ds(c * LANES, LANES)
        wait_bytes(all_but_mine(inc, c), x_recv.at[c])
        terms = three_parts(inc[c])

        def add_in(i, _):
            part = pl.ds(pl.multiple_of(i * 256, 256), 256)
            totals = partial[part, lanes] + add_parts(dot(scat[part, :], terms))
            aggr[part, lanes] = totals.astype(BF16)
            return 0

        lax.fori_loop(0, masters // 256, add_in, 0)
        rounded = aggr[pl.ds(0, masters), lanes]

        def reply(i, _):
            part = pl.ds(pl.multiple_of(i * 256, 256), 256)
            rep[c, part, :] = dot(take[part, :], rounded)
            return 0

        lax.fori_loop(0, total_slots // 256, reply, 0)
        exchange(rep, ans, c, x_send.at[CHUNKS + c], x_recv.at[CHUNKS + c])

    contract_rows = (((0,), (0,)), ((), ()))
    g[...] = jnp.zeros_like(g)

    def early(i, _):
        part = pl.ds(pl.multiple_of(i * 256, 256), 256)
        features = nf[pl.ds(2 * i, 2)].reshape(2 * tile, feat)
        rounded = aggr[part, :]
        preact = dot(features, ws[...]) + dot(rounded, wn[...])
        out[part, :] = jnp.maximum(preact, 0.0).astype(BF16)
        kept = jnp.where(preact > 0, cot[part, :], jnp.zeros((256, feat), BF16))
        for c in range(CHUNKS):
            side = kept[:, c * LANES : (c + 1) * LANES]
            g[c, pl.ds(0, feat), :] += lax.dot_general(features, side, contract_rows, preferred_element_type=F32)
            g[c, pl.ds(feat, feat), :] += lax.dot_general(rounded, side, contract_rows, preferred_element_type=F32)
        return 0

    lax.fori_loop(0, masters // 256, early, 0)
    end = pl.ds(masters, late)
    features = nf[pl.ds(masters // tile, late // tile)].reshape(late, feat)
    pre[...] = dot(features, ws[...])
    lhs[pl.ds(0, feat), :] = features.T

    for c in range(CHUNKS):
        lanes = pl.ds(c * LANES, LANES)
        wait_bytes(all_but_mine(ans, c), x_recv.at[CHUNKS + c])
        placed = dot(place[...], ans[c].astype(BF16))
        rounded = jnp.where(live_row[...] > 0, placed, partial[end, lanes]).astype(BF16)
        pre[...] += dot(rounded, wn[pl.ds(c * LANES, LANES), :])
        lhs[pl.ds(feat + c * LANES, LANES), :] = rounded.T

    half, x_rows = feat, feat // NX
    y_rows = x_rows // NY
    own = pl.ds(pl.multiple_of(core * half, half), half)
    other = pl.ds(pl.multiple_of((1 - core) * half, half), half)
    x_own = pl.ds(pl.multiple_of(x * x_rows, x_rows), x_rows)
    y_own = pl.ds(pl.multiple_of(y * y_rows, y_rows), y_rows)

    def copy_to(src, dst, stage, c, device):
        pltpu.make_async_remote_copy(
            src_ref=src, dst_ref=dst, send_sem=r_send.at[stage, c], recv_sem=r_recv.at[stage, c],
            device_id=device, device_id_type=MESH,
        ).start()

    for c in range(CHUNKS):
        lanes = pl.ds(c * LANES, LANES)
        preact = pre[:, lanes]
        out[end, lanes] = jnp.maximum(preact, 0.0).astype(BF16)
        kept = jnp.where(preact > 0, cot[end, lanes], jnp.zeros((late, LANES), BF16))
        g[c] = g[c] + dot(lhs[...], kept)
        copy_to(g.at[c, other], b0.at[c], 0, c, partner)
    for c in range(CHUNKS):
        wait_bytes(b0.at[c], r_recv.at[0, c])
        acc[c] = g[c, own, :] + b0[c]
        for k in (2, 1, 3):
            part = pl.ds(pl.multiple_of(lax.rem(x + k, NX) * x_rows, x_rows), x_rows)
            copy_to(acc.at[c, part], b1.at[c, k - 1], 1, c, x_peer(k))
    for c in range(CHUNKS):
        wait_bytes(b1.at[c], r_recv.at[1, c])
        acc1[c] = acc[c, x_own, :] + b1[c, 0] + b1[c, 1] + b1[c, 2]
        for k in (4, 3, 5, 2, 6, 1, 7):
            part = pl.ds(pl.multiple_of(lax.rem(y + k, NY) * y_rows, y_rows), y_rows)
            copy_to(acc1.at[c, part], b2.at[c, k - 1], 2, c, y_peer(k))
    for c in range(CHUNKS):
        wait_bytes(b2.at[c], r_recv.at[2, c])
        total = acc1[c, y_own, :]
        for k in range(NY - 1):
            total = total + b2[c, k]
        acc2[c] = total
        for k in (6, 5, 7, 4, 8, 3, 9, 2, 10, 1, 11):
            copy_to(acc2.at[c], b3.at[c, z], 3, c, z_peer(k))
        b3[c, z] = total
    at = pl.ds(pl.multiple_of(core * half + x * x_rows + y * y_rows, y_rows), y_rows)
    x_block = pl.ds(pl.multiple_of(core * half + x * x_rows, x_rows), x_rows)
    for c in range(CHUNKS):
        lanes = pl.ds(c * LANES, LANES)
        wait_bytes(b3.at[c, pl.ds(0, NZ - 1)], r_recv.at[3, c])
        total = b3[c, 0]
        for k in range(1, NZ):
            total = total + b3[c, k]
        grad[at, lanes] = total * factor
        for k in (4, 3, 5, 2, 6, 1, 7):
            copy_to(grad.at[at, lanes], grad.at[at, lanes], 4, c, y_peer(k))
    for c in range(CHUNKS):
        lanes = pl.ds(c * LANES, LANES)
        wait_bytes(grad.at[pl.ds(0, y_rows * (NY - 1)), lanes], r_recv.at[4, c])
        for k in (2, 1, 3):
            copy_to(grad.at[x_block, lanes], grad.at[x_block, lanes], 5, c, x_peer(k))
    for c in range(CHUNKS):
        lanes = pl.ds(c * LANES, LANES)
        wait_bytes(grad.at[pl.ds(0, x_rows * (NX - 1)), lanes], r_recv.at[5, c])
        copy_to(grad.at[own, lanes], grad.at[own, lanes], 6, c, partner)
    for c in range(CHUNKS):
        lanes = pl.ds(c * LANES, LANES)
        wait_bytes(grad.at[own, lanes], r_recv.at[6, c])
        for n, ref in enumerate((
            b0.at[c], b1.at[c], b2.at[c], b3.at[c, pl.ds(0, NZ - 1)], grad.at[pl.ds(0, y_rows * (NY - 1)), lanes],
            grad.at[pl.ds(0, x_rows * (NX - 1)), lanes], grad.at[own, lanes],
        )):
            wait_bytes(ref, r_send.at[n, c])
        wait_bytes(all_but_mine(inc, c), x_send.at[c])
        wait_bytes(all_but_mine(ans, c), x_send.at[CHUNKS + c])
    self_grad[...] = grad[pl.ds(0, feat), :]
    neighbor_grad[...] = grad[pl.ds(feat, feat), :]


def shards(
    node_features,
    edge_blocks,
    block_target,
    block_source,
    block_count,
    replica_rows,
    master_rows,
    send_counts,
    bin_delay,
    past_partials,
    self_weight,
    neighbor_weight,
    output_cotangent,
):
    nodes, feat = node_features.shape
    _, peers, slots = replica_rows.shape
    total_slots = peers * slots
    masters = nodes - total_slots
    late = total_slots
    tiles = nodes // edge_blocks.shape[1]
    history = past_partials[0].reshape(past_partials.shape[1], total_slots, feat)
    factor = 1.0 / math.sqrt(nodes * lax.axis_size("dom") * lax.axis_size("grp"))

    vmem = pl.BlockSpec(memory_space=pltpu.VMEM)
    hbm = pl.BlockSpec(memory_space=pl.ANY)
    blocks, tile = edge_blocks.shape[:2]
    bins = bin_delay.shape[2]
    x_rows = feat // NX
    y_rows = x_rows // NY
    big = (CHUNKS, total_slots, LANES)
    v = pltpu.VMEM
    return pl.pallas_call(
        functools.partial(layer_kernel, factor, masters),
        out_shape=(
            jax.ShapeDtypeStruct((nodes, feat), BF16),
            jax.ShapeDtypeStruct((feat, feat), F32),
            jax.ShapeDtypeStruct((feat, feat), F32),
        ),
        in_specs=[hbm] * 9 + [pl.BlockSpec(memory_space=pltpu.SMEM)] + [hbm] * 3,
        out_specs=(vmem, vmem, vmem),
        scratch_shapes=[
            pltpu.SMEM((1, blocks), jnp.int32), v((tiles, tile, feat), BF16), v(edge_blocks.shape, BF16), v(history.shape, BF16),
            v((slots, peers), jnp.int32), v((slots, peers), jnp.int32), v((1, peers), jnp.int32), v((bins, peers), jnp.int32),
            v((1, blocks), jnp.int32),
            v((feat, feat), BF16), v((feat, feat), BF16), v((nodes, feat), BF16),
            v((tiles, blocks), F32), v((total_slots, 8), F32), v((8, total_slots), F32),
            v((blocks, tile, feat), F32), v((nodes, feat), F32),
            v((total_slots, late), BF16), v((masters, total_slots), BF16), v((total_slots, masters), BF16),
            v((late, total_slots), BF16), v((late, LANES), F32),
            v(big, F32), v(big, F32), v(big, F32), v(big, F32), v((nodes, feat), BF16),
            v((late, feat), F32), v((2 * feat, late), BF16),
            v((CHUNKS, 2 * feat, LANES), F32), v((CHUNKS, feat, LANES), F32), v((CHUNKS, feat, LANES), F32),
            v((CHUNKS, NX - 1, x_rows, LANES), F32), v((CHUNKS, x_rows, LANES), F32),
            v((CHUNKS, NY - 1, y_rows, LANES), F32), v((CHUNKS, y_rows, LANES), F32),
            v((CHUNKS, NZ, y_rows, LANES), F32), v((2 * feat, feat), F32),
            pltpu.SemaphoreType.DMA((12,)), pltpu.SemaphoreType.DMA((2 * CHUNKS,)), pltpu.SemaphoreType.DMA((2 * CHUNKS,)),
            pltpu.SemaphoreType.DMA((7, CHUNKS)), pltpu.SemaphoreType.DMA((7, CHUNKS)),
        ],
        compiler_params=pltpu.CompilerParams(
            collective_id=0, has_side_effects=True, vmem_limit_bytes=40 * 2**20
        ),
        name="layer",
    )(
        *(
            pltpu.with_memory_space_constraint(a, pltpu.HBM) if a.ndim > 1 else a
            for a in (
                block_source, node_features.reshape(tiles, tile, feat), edge_blocks, history, replica_rows[0].T, master_rows[0].T,
                send_counts, bin_delay[0].T, block_target, block_count,
                self_weight, neighbor_weight, output_cotangent,
            )
        ),
    )


def solution(mesh):
    return jax.shard_map(
        shards,
        mesh=mesh,
        in_specs=(
            P(("dom", "grp"), None),
            P(("dom", "grp"), None, None),
            P(("dom", "grp"), None),
            P(("dom", "grp"), None),
            P(("dom", "grp")),
            P(("dom", "grp"), None, None),
            P(("dom", "grp"), None, None),
            P(("dom", "grp"), None),
            P(("dom", "grp"), None, None),
            P(("dom", "grp"), None, None, None, None),
            P(),
            P(),
            P(("dom", "grp"), None),
        ),
        out_specs=(P(("dom", "grp"), None), P(), P()),
        check_vma=False,
    )
```

```python
import functools
import math

import jax
import jax.numpy as jnp
from jax import lax
from jax.experimental import pallas as pl
from jax.experimental.pallas import tpu as pltpu
from jax.sharding import PartitionSpec as P

MESH = pl.DeviceIdType.MESH
F32 = jnp.float32
BF16 = jnp.bfloat16
NX, NY, NZ = 4, 8, 12
LANES = 128
CHUNKS = 2


def three_parts(x):
    high = x.astype(BF16)
    rest = x - high.astype(F32)
    middle = rest.astype(BF16)
    low = (rest - middle.astype(F32)).astype(BF16)
    return jnp.concatenate([high, middle, low], axis=1)


def add_parts(d):
    return d[:, :LANES] + d[:, LANES : 2 * LANES] + d[:, 2 * LANES :]


def one_hot(hit):
    return jnp.where(hit, 1.0, 0.0).astype(BF16)


def dot(a, b):
    return jnp.dot(a, b, preferred_element_type=F32)


def wait_bytes(ref, sem):
    pltpu.make_async_copy(ref, ref, sem).wait()


def layer_kernel(
    factor, masters,
    source_h, nf_h, eb_h, hist_h, rep_h, mas_h, sent_h, delay_h, target_h, count, ws_h, wn_h, cot_h,
    out, grads,
    source, nf, eb, hist, replica, master, sent, delay, target, ws, wn, cot, weight, cols, rows,
    prod, partial, pick, scat, take, place, live_row, outg, inc, rep, ans, aggr,
    pre, lhs, g, b0, acc, b1, acc1, b2, acc2, b3, grad,
    in_sem, x_send, x_recv, r_send, r_recv,
):
    dom = lax.axis_index("dom")
    grp = lax.axis_index("grp")
    x, z, y, core = dom // NZ, lax.rem(dom, NZ), grp // 2, lax.rem(grp, 2)
    peers = NX * NZ
    slots = cols.shape[0] // peers
    total_slots = cols.shape[0]
    tiles, tile, feat = nf.shape
    nodes = tiles * tile
    late = nodes - masters
    blocks = eb.shape[0]

    def x_peer(k):
        return (lax.rem(x + k, NX) * NZ + z, grp)

    def y_peer(k):
        return (dom, lax.rem(y + k, NY) * 2 + core)

    def z_peer(k):
        return (x * NZ + lax.rem(z + k, NZ), grp)

    partner = (dom, y * 2 + 1 - core)

    pairs = (
        (rep_h, replica), (mas_h, master), (sent_h, sent), (delay_h, delay), (target_h, target), (source_h, source),
        (eb_h, eb), (nf_h, nf), (hist_h, hist), (ws_h, ws), (wn_h, wn), (cot_h, cot),
    )
    loads = [pltpu.make_async_copy(a, b, in_sem.at[n]) for n, (a, b) in enumerate(pairs)]
    for copy in loads[:8]:
        copy.start()
    barrier = pltpu.get_barrier_semaphore()

    def greet(device):
        pl.semaphore_signal(barrier, inc=1, device_id=device, device_id_type=MESH)

    def greet_dom(k, _):
        greet((lax.rem(dom + k, peers), grp))
        return 0

    lax.fori_loop(1, peers, greet_dom, 0)
    for k in range(1, NY):
        greet(y_peer(k))
    greet(partner)

    for copy in loads[:5]:
        copy.wait()

    shift = slots.bit_length() - 1

    spread = one_hot(
        lax.broadcasted_iota(jnp.int32, (peers, total_slots), 1) >> shift
        == lax.broadcasted_iota(jnp.int32, (peers, total_slots), 0)
    )
    here = lax.broadcasted_iota(jnp.int32, (slots, total_slots), 1) & (slots - 1) == lax.broadcasted_iota(
        jnp.int32, (slots, total_slots), 0
    )

    def flat(ref):
        high = dot((ref[...] >> 4).astype(F32).astype(BF16), spread)
        low = dot((ref[...] & 15).astype(F32).astype(BF16), spread)
        return jnp.sum(jnp.where(here, high * 16.0 + low, 0.0), axis=0, keepdims=True)

    replica_row, master_row = flat(replica), flat(master)
    sent_row = dot(sent[...].astype(F32).astype(BF16), spread)
    delays = dot(delay[...].astype(F32).astype(BF16), spread)
    slot = lax.broadcasted_iota(jnp.int32, (1, total_slots), 1) & (slots - 1)
    bins = delay.shape[0]
    delay_row = delays[0:1]
    for n in range(1, bins):
        delay_row = jnp.where(slot >= n * (slots // bins), delays[n : n + 1], delay_row)
    live = slot.astype(F32) < sent_row
    rows[0:1, :] = jnp.where(live & (delay_row == 0.0), replica_row, -1.0)
    rows[1:2, :] = jnp.where(live, replica_row, -1.0)
    rows[2:3, :] = jnp.where(live, delay_row, 0.0)
    rows[3:4, :] = master_row
    rows[4:8, :] = jnp.zeros((4, total_slots), F32)
    cols[...] = rows[...].T

    def make_pick(i, _):
        part = pl.ds(pl.multiple_of(i * LANES, LANES), LANES)
        number = (lax.broadcasted_iota(jnp.int32, (LANES, late), 1) + masters).astype(F32)
        pick[part, :] = one_hot(cols[part, 0:1] == number)
        return 0

    lax.fori_loop(0, total_slots // LANES, make_pick, 0)

    used = lax.broadcasted_iota(jnp.int32, (tiles, blocks), 1) < count[0]
    into = lax.broadcasted_iota(jnp.int32, (tiles, blocks), 0) == target[...]
    weight[...] = jnp.where(used & into, 1.0, 0.0)
    for copy in loads[5:8]:
        copy.wait()
    for copy in loads[8:]:
        copy.start()

    def multiply(b, _):
        prod[b] = dot(eb[b], nf[source[0, b]])
        return 0

    lax.fori_loop(0, blocks, multiply, 0, unroll=True)
    def collect(t, _):
        total = jnp.zeros((tile, feat), F32)
        for b in range(blocks):
            total = total + weight[pl.ds(t, 1), pl.ds(b, 1)] * prod[b]
        partial[pl.ds(pl.multiple_of(t * tile, tile), tile), :] = total
        return 0

    lax.fori_loop(masters // tile, nodes // tile, collect, 0)
    def fill(c):
        lanes = pl.ds(c * LANES, LANES)
        terms = three_parts(partial[pl.ds(masters, late), lanes])

        def piece(i, _):
            part = pl.ds(pl.multiple_of(i * 256, 256), 256)
            fresh = add_parts(dot(pick[part, :], terms))
            age = cols[part, 2:3]
            stale = jnp.where(age == 1, hist[0, part, lanes].astype(F32), 0.0)
            stale = jnp.where(age == 2, hist[1, part, lanes].astype(F32), stale)
            outg[c, part, :] = fresh + stale
            return 0

        lax.fori_loop(0, total_slots // 256, piece, 0)

    def exchange(from_ref, to_ref, c, send, recv):
        mine = pl.ds(pl.multiple_of(dom * slots, slots), slots)

        def start(i, _):
            step, dx = i // NX, NX - 1 - lax.rem(i, NX)
            off = (step + 1) // 2
            dz = NZ // 2 + off * (2 * lax.rem(step, 2) - 1)
            peer = lax.rem(x + dx, NX) * NZ + lax.rem(z + dz, NZ)
            pltpu.make_async_remote_copy(
                src_ref=from_ref.at[c, pl.ds(pl.multiple_of(peer * slots, slots), slots)],
                dst_ref=to_ref.at[c, mine],
                send_sem=send,
                recv_sem=recv,
                device_id=(peer, grp),
                device_id_type=MESH,
            ).start()
            return 0

        lax.fori_loop(0, peers - 1, start, 0)
        to_ref[c, mine, :] = from_ref[c, mine, :]

    def all_but_mine(ref, c):
        return ref.at[c, pl.ds(0, total_slots - slots)]

    loads[8].wait()
    fill(0)
    pl.semaphore_wait(barrier, peers - 1 + NY - 1 + 1)
    exchange(outg, inc, 0, x_send.at[0], x_recv.at[0])
    fill(1)
    exchange(outg, inc, 1, x_send.at[1], x_recv.at[1])

    lax.fori_loop(0, masters // tile, collect, 0)
    for copy in loads[9:]:
        copy.wait()

    def make_scat(i, _):
        part = pl.ds(pl.multiple_of(i * LANES, LANES), LANES)
        number = (lax.broadcasted_iota(jnp.int32, (LANES, total_slots), 0) + i * LANES).astype(F32)
        scat[part, :] = one_hot(rows[3:4, :] == number)
        return 0

    lax.fori_loop(0, masters // LANES, make_scat, 0)

    def make_take(i, _):
        part = pl.ds(pl.multiple_of(i * LANES, LANES), LANES)
        number = lax.broadcasted_iota(jnp.int32, (LANES, masters), 1).astype(F32)
        take[part, :] = one_hot(cols[part, 3:4] == number)
        return 0

    lax.fori_loop(0, total_slots // LANES, make_take, 0)

    def make_place(i, _):
        part = pl.ds(pl.multiple_of(i * LANES, LANES), LANES)
        number = (lax.broadcasted_iota(jnp.int32, (LANES, total_slots), 0) + i * LANES + masters).astype(F32)
        hits = one_hot(rows[1:2, :] == number)
        place[part, :] = hits
        live_row[part, :] = dot(hits, jnp.ones((total_slots, LANES), BF16))
        return 0

    lax.fori_loop(0, late // LANES, make_place, 0)

    for c in range(CHUNKS):
        lanes = pl.ds(c * LANES, LANES)
        wait_bytes(all_but_mine(inc, c), x_recv.at[c])
        terms = three_parts(inc[c])

        def add_in(i, _):
            part = pl.ds(pl.multiple_of(i * 256, 256), 256)
            totals = partial[part, lanes] + add_parts(dot(scat[part, :], terms))
            aggr[part, lanes] = totals.astype(BF16)
            return 0

        lax.fori_loop(0, masters // 256, add_in, 0)
        rounded = aggr[pl.ds(0, masters), lanes]

        def reply(i, _):
            part = pl.ds(pl.multiple_of(i * 256, 256), 256)
            rep[c, part, :] = dot(take[part, :], rounded)
            return 0

        lax.fori_loop(0, total_slots // 256, reply, 0)
        exchange(rep, ans, c, x_send.at[CHUNKS + c], x_recv.at[CHUNKS + c])

    contract_rows = (((0,), (0,)), ((), ()))
    g[...] = jnp.zeros_like(g)

    def early(i, _):
        part = pl.ds(pl.multiple_of(i * 256, 256), 256)
        features = nf[pl.ds(2 * i, 2)].reshape(2 * tile, feat)
        rounded = aggr[part, :]
        preact = dot(features, ws[...]) + dot(rounded, wn[...])
        out[part, :] = jnp.maximum(preact, 0.0).astype(BF16)
        kept = jnp.where(preact > 0, cot[part, :], jnp.zeros((256, feat), BF16))
        for c in range(CHUNKS):
            side = kept[:, c * LANES : (c + 1) * LANES]
            g[c, pl.ds(0, feat), :] += lax.dot_general(features, side, contract_rows, preferred_element_type=F32)
            g[c, pl.ds(feat, feat), :] += lax.dot_general(rounded, side, contract_rows, preferred_element_type=F32)
        return 0

    lax.fori_loop(0, masters // 256, early, 0)
    end = pl.ds(masters, late)
    features = nf[pl.ds(masters // tile, late // tile)].reshape(late, feat)
    pre[...] = dot(features, ws[...])
    lhs[pl.ds(0, feat), :] = features.T

    for c in range(CHUNKS):
        lanes = pl.ds(c * LANES, LANES)
        wait_bytes(all_but_mine(ans, c), x_recv.at[CHUNKS + c])
        placed = dot(place[...], ans[c].astype(BF16))
        rounded = jnp.where(live_row[...] > 0, placed, partial[end, lanes]).astype(BF16)
        pre[...] += dot(rounded, wn[pl.ds(c * LANES, LANES), :])
        lhs[pl.ds(feat + c * LANES, LANES), :] = rounded.T

    half, x_rows = feat, feat // NX
    y_rows = x_rows // NY
    own = pl.ds(pl.multiple_of(core * half, half), half)
    other = pl.ds(pl.multiple_of((1 - core) * half, half), half)
    x_own = pl.ds(pl.multiple_of(x * x_rows, x_rows), x_rows)
    y_own = pl.ds(pl.multiple_of(y * y_rows, y_rows), y_rows)

    def copy_to(src, dst, stage, c, device):
        pltpu.make_async_remote_copy(
            src_ref=src, dst_ref=dst, send_sem=r_send.at[stage, c], recv_sem=r_recv.at[stage, c],
            device_id=device, device_id_type=MESH,
        ).start()

    for c in range(CHUNKS):
        lanes = pl.ds(c * LANES, LANES)
        preact = pre[:, lanes]
        out[end, lanes] = jnp.maximum(preact, 0.0).astype(BF16)
        kept = jnp.where(preact > 0, cot[end, lanes], jnp.zeros((late, LANES), BF16))
        g[c] = g[c] + dot(lhs[...], kept)
        copy_to(g.at[c, other], b0.at[c], 0, c, partner)
    for c in range(CHUNKS):
        wait_bytes(b0.at[c], r_recv.at[0, c])
        acc[c] = g[c, own, :] + b0[c]
        for k in (2, 1, 3):
            part = pl.ds(pl.multiple_of(lax.rem(x + k, NX) * x_rows, x_rows), x_rows)
            copy_to(acc.at[c, part], b1.at[c, k - 1], 1, c, x_peer(k))
    for c in range(CHUNKS):
        wait_bytes(b1.at[c], r_recv.at[1, c])
        acc1[c] = acc[c, x_own, :] + b1[c, 0] + b1[c, 1] + b1[c, 2]
        for k in (4, 3, 5, 2, 6, 1, 7):
            part = pl.ds(pl.multiple_of(lax.rem(y + k, NY) * y_rows, y_rows), y_rows)
            copy_to(acc1.at[c, part], b2.at[c, k - 1], 2, c, y_peer(k))
    for c in range(CHUNKS):
        wait_bytes(b2.at[c], r_recv.at[2, c])
        total = acc1[c, y_own, :]
        for k in range(NY - 1):
            total = total + b2[c, k]
        acc2[c] = total
        for k in (6, 5, 7, 4, 8, 3, 9, 2, 10, 1, 11):
            copy_to(acc2.at[c], b3.at[c, z], 3, c, z_peer(k))
        b3[c, z] = total
    at = pl.ds(pl.multiple_of(core * half + x * x_rows + y * y_rows, y_rows), y_rows)
    x_block = pl.ds(pl.multiple_of(core * half + x * x_rows, x_rows), x_rows)
    for c in range(CHUNKS):
        lanes = pl.ds(c * LANES, LANES)
        wait_bytes(b3.at[c, pl.ds(0, NZ - 1)], r_recv.at[3, c])
        total = b3[c, 0]
        for k in range(1, NZ):
            total = total + b3[c, k]
        grad[at, lanes] = total * factor
        for k in (4, 3, 5, 2, 6, 1, 7):
            copy_to(grad.at[at, lanes], grad.at[at, lanes], 4, c, y_peer(k))
    for c in range(CHUNKS):
        lanes = pl.ds(c * LANES, LANES)
        wait_bytes(grad.at[pl.ds(0, y_rows * (NY - 1)), lanes], r_recv.at[4, c])
        for k in (2, 1, 3):
            copy_to(grad.at[x_block, lanes], grad.at[x_block, lanes], 5, c, x_peer(k))
    for c in range(CHUNKS):
        lanes = pl.ds(c * LANES, LANES)
        wait_bytes(grad.at[pl.ds(0, x_rows * (NX - 1)), lanes], r_recv.at[5, c])
        copy_to(grad.at[own, lanes], grad.at[own, lanes], 6, c, partner)
    for c in range(CHUNKS):
        lanes = pl.ds(c * LANES, LANES)
        wait_bytes(grad.at[own, lanes], r_recv.at[6, c])
        for n, ref in enumerate((
            b0.at[c], b1.at[c], b2.at[c], b3.at[c, pl.ds(0, NZ - 1)], grad.at[pl.ds(0, y_rows * (NY - 1)), lanes],
            grad.at[pl.ds(0, x_rows * (NX - 1)), lanes], grad.at[own, lanes],
        )):
            wait_bytes(ref, r_send.at[n, c])
        wait_bytes(all_but_mine(inc, c), x_send.at[c])
        wait_bytes(all_but_mine(ans, c), x_send.at[CHUNKS + c])
    grads[0] = grad[pl.ds(0, feat), :]
    grads[1] = grad[pl.ds(feat, feat), :]


def shards(
    node_features,
    edge_blocks,
    block_target,
    block_source,
    block_count,
    replica_rows,
    master_rows,
    send_counts,
    bin_delay,
    past_partials,
    self_weight,
    neighbor_weight,
    output_cotangent,
):
    nodes, feat = node_features.shape
    _, peers, slots = replica_rows.shape
    total_slots = peers * slots
    masters = nodes - total_slots
    late = total_slots
    tiles = nodes // edge_blocks.shape[1]
    history = past_partials[0].reshape(past_partials.shape[1], total_slots, feat)
    factor = 1.0 / math.sqrt(nodes * lax.axis_size("dom") * lax.axis_size("grp"))

    vmem = pl.BlockSpec(memory_space=pltpu.VMEM)
    hbm = pl.BlockSpec(memory_space=pl.ANY)
    blocks, tile = edge_blocks.shape[:2]
    bins = bin_delay.shape[2]
    x_rows = feat // NX
    y_rows = x_rows // NY
    big = (CHUNKS, total_slots, LANES)
    v = pltpu.VMEM
    out, grads = pl.pallas_call(
        functools.partial(layer_kernel, factor, masters),
        out_shape=(
            jax.ShapeDtypeStruct((nodes, feat), BF16),
            jax.ShapeDtypeStruct((2, feat, feat), F32),
        ),
        in_specs=[hbm] * 9 + [pl.BlockSpec(memory_space=pltpu.SMEM)] + [hbm] * 3,
        out_specs=(vmem, vmem),
        scratch_shapes=[
            pltpu.SMEM((1, blocks), jnp.int32), v((tiles, tile, feat), BF16), v(edge_blocks.shape, BF16), v(history.shape, BF16),
            v((slots, peers), jnp.int32), v((slots, peers), jnp.int32), v((1, peers), jnp.int32), v((bins, peers), jnp.int32),
            v((1, blocks), jnp.int32),
            v((feat, feat), BF16), v((feat, feat), BF16), v((nodes, feat), BF16),
            v((tiles, blocks), F32), v((total_slots, 8), F32), v((8, total_slots), F32),
            v((blocks, tile, feat), F32), v((nodes, feat), F32),
            v((total_slots, late), BF16), v((masters, total_slots), BF16), v((total_slots, masters), BF16),
            v((late, total_slots), BF16), v((late, LANES), F32),
            v(big, F32), v(big, F32), v(big, F32), v(big, F32), v((nodes, feat), BF16),
            v((late, feat), F32), v((2 * feat, late), BF16),
            v((CHUNKS, 2 * feat, LANES), F32), v((CHUNKS, feat, LANES), F32), v((CHUNKS, feat, LANES), F32),
            v((CHUNKS, NX - 1, x_rows, LANES), F32), v((CHUNKS, x_rows, LANES), F32),
            v((CHUNKS, NY - 1, y_rows, LANES), F32), v((CHUNKS, y_rows, LANES), F32),
            v((CHUNKS, NZ, y_rows, LANES), F32), v((2 * feat, feat), F32),
            pltpu.SemaphoreType.DMA((12,)), pltpu.SemaphoreType.DMA((2 * CHUNKS,)), pltpu.SemaphoreType.DMA((2 * CHUNKS,)),
            pltpu.SemaphoreType.DMA((7, CHUNKS)), pltpu.SemaphoreType.DMA((7, CHUNKS)),
        ],
        compiler_params=pltpu.CompilerParams(
            collective_id=0, has_side_effects=True, vmem_limit_bytes=40 * 2**20
        ),
        name="layer",
    )(
        *(
            pltpu.with_memory_space_constraint(a, pltpu.HBM) if a.ndim > 1 else a
            for a in (
                block_source, node_features.reshape(tiles, tile, feat), edge_blocks, history, replica_rows[0].T, master_rows[0].T,
                send_counts, bin_delay[0].T, block_target, block_count,
                self_weight, neighbor_weight, output_cotangent,
            )
        ),
    )
    return (out, grads[0], grads[1])


def solution(mesh):
    return jax.shard_map(
        shards,
        mesh=mesh,
        in_specs=(
            P(("dom", "grp"), None),
            P(("dom", "grp"), None, None),
            P(("dom", "grp"), None),
            P(("dom", "grp"), None),
            P(("dom", "grp")),
            P(("dom", "grp"), None, None),
            P(("dom", "grp"), None, None),
            P(("dom", "grp"), None),
            P(("dom", "grp"), None, None),
            P(("dom", "grp"), None, None, None, None),
            P(),
            P(),
            P(("dom", "grp"), None),
        ),
        out_specs=(P(("dom", "grp"), None), P(), P()),
        check_vma=False,
    )
```
